32 devices in a mesh: groups: 2 (over x), dom: 16 (over z, y, core).
Axes of the slice: x: 2, y: 2, z: 4, core: 2. Of those that a mesh axis runs over, the one named last changes fastest.
Arguments:
- features: bfloat16 [262144, 128], P(('groups', 'dom')), parts along dimension 0, may hold values from -6 to 6
- stale_features: bfloat16 [262144, 128], P(('groups', 'dom')), parts along dimension 0, may hold values from -6 to 6
- stale_grads: bfloat16 [32768, 128], P(('groups', 'dom')), parts along dimension 0, may hold values from -2 to 2
- send_rows: int32 [256, 128], P(('groups', 'dom')), parts along dimension 0, may hold values from 0 to 8191
- send_count: int32 [32, 8], P(('groups', 'dom')), parts along dimension 0, may hold values from 32 to 128, as said below
- tile_block: int32 [2048, 4], P(('groups', 'dom')), parts along dimension 0, may hold values from 0 to 71
- neighbor_slot: int32 [262144, 8], P(('groups', 'dom')), parts along dimension 0, may hold values from 0 to 511
- labels: int32 [262144], P(('groups', 'dom')), parts along dimension 0, may hold values from 0 to 12
- w_self: bfloat16 [128, 128], replicated, may hold values from -0.5 to 0.5
- w_neigh: bfloat16 [128, 128], replicated, may hold values from -0.5 to 0.5
- bias: float32 [128], replicated, may hold values from -4 to 4
- w_cls: bfloat16 [128, 13], replicated, may hold values from -0.5 to 0.5
Outputs:
- grad_features: float32 [262144, 128], P(('groups', 'dom')), parts along dimension 0
- halo_grad: float32 [32768, 128], P(('groups', 'dom')), parts along dimension 0
- grad_w_self: float32 [256, 128], P('groups'), parts along dimension 0
- grad_w_neigh: float32 [256, 128], P('groups'), parts along dimension 0
- grad_bias: float32 [256], P('groups'), parts along dimension 0
- grad_w_cls: float32 [256, 13], P('groups'), parts along dimension 0
The draws below stay inside these ranges and needn't reach their ends.
There are 2 independent parts, one for each index of `groups`. The reference program is written for one: setup_inputs(seed, part) draws one part's arguments, and reference() takes and returns one part's arrays. A program takes and returns all parts, laid end to end along the dimension named above; an argument that names none is the same for every part. Nothing has to cross between parts.
Inputs may be any that keep to these rules, and one draw needn't show every extreme that they name: `send_count`: every partition sends exactly 128 rows in one of its send lists; every list has at least 32 live entries.
All inputs are finite; a program needn't handle non-finite values.
Results may differ from the reference program's by a relative error of at most 0.0039.
Values may be sent and summed in bfloat16 or wider, within the bound.
A program may use at most 128 MiB of HBM per device.

```python
import math
import jax
import jax.numpy as jnp
from jax import lax

F = 128
C = 13
V_DEV = 8192
BLOCK = 128
TILES = 4
K = 8
NOFF = 8
CAP = 128
VOXELS = 131072
BLOCKS = 64
EXT_BLOCKS = 72
HALO = 16384
LISTS = 128
N_DOM = 16


def draw_send_count(key, part):
    key = jax.random.fold_in(key, 7)
    counts = jax.random.randint(key, (N_DOM, NOFF), CAP // 4, CAP + 1)
    full_slot = jnp.arange(N_DOM, dtype=jnp.int32) % NOFF
    chosen = jnp.arange(NOFF, dtype=jnp.int32)[None, :] == full_slot[:, None]
    return jnp.where(chosen, CAP, counts).astype(jnp.int32)


def place_ends(result, rng, least, top_value):
    index_at = [jax.random.randint(jax.random.fold_in(rng, axis), (), 0, length) for axis, length in enumerate(result.shape)]
    longest = result.shape.index(max(result.shape))
    beside = index_at[:longest] + [(index_at[longest] + 1) % result.shape[longest]] + index_at[longest + 1:]
    return result.at[tuple(index_at)].set(least).at[tuple(beside)].set(top_value)


def level_of(rng, shape, shards, low, largest):
    def one(position, blocks):
        steps = jax.random.uniform(jax.random.fold_in(jax.random.fold_in(rng, 6), position), (blocks,), jnp.float32, low / len(shards), largest / len(shards))
        return jnp.repeat(jnp.exp(steps), shape[position] // blocks).reshape((-1,) + (1,) * (len(shape) - position - 1))

    gain = one(*shards[0])
    for cut in shards[1:]:
        gain = gain * one(*cut)
    return gain


def scatter_about(own_key, dims, spread, most, cuts=(), held_as=jnp.bfloat16):
    values = spread * jax.random.normal(own_key, dims, jnp.float32)
    if cuts:
        values = values * level_of(own_key, dims, cuts, -0.22, 0.18)
    return jnp.clip(values, -most, most).astype(held_as)


def setup_inputs(seed: int = 0, part: int = 0) -> dict:
    key_of = jax.random.split(jax.random.key(seed), 13)
    part_keys = jax.random.split(jax.random.fold_in(key_of[12], part), 13)
    return {
        "features": scatter_about(part_keys[0], (VOXELS, F), 1.0, 6.0, ((0, 16),)),
        "stale_features": scatter_about(part_keys[1], (VOXELS, F), 1.0, 6.0, ((0, 16),)),
        "stale_grads": scatter_about(part_keys[2], (HALO, F), 0.3, 2.0, ((0, 16),)),
        "send_rows": place_ends(jax.random.randint(part_keys[3], (LISTS, CAP), 0, V_DEV), jax.random.fold_in(part_keys[3], 1), 0, V_DEV - 1).astype(jnp.int32),
        "send_count": draw_send_count(jax.random.fold_in(jax.random.fold_in(key_of[12], part), 71), part),
        "tile_block": place_ends(jax.random.randint(part_keys[5], (VOXELS // BLOCK, TILES), 0, EXT_BLOCKS), jax.random.fold_in(part_keys[5], 1), 0, EXT_BLOCKS - 1).astype(jnp.int32),
        "neighbor_slot": place_ends(jax.random.randint(part_keys[6], (VOXELS, K), 0, TILES * BLOCK), jax.random.fold_in(part_keys[6], 1), 0, (TILES * BLOCK) - 1).astype(jnp.int32),
        "labels": place_ends(jax.random.randint(part_keys[7], (VOXELS,), 0, C), jax.random.fold_in(part_keys[7], 1), 0, C - 1).astype(jnp.int32),
        "w_self": scatter_about(key_of[8], (F, F), F ** -0.5, 0.5),
        "w_neigh": scatter_about(key_of[9], (F, F), F ** -0.5, 0.5),
        "bias": scatter_about(key_of[10], (F,), 1.0, 4.0, (), jnp.float32),
        "w_cls": scatter_about(key_of[11], (F, C), F ** -0.5, 0.5),
    }


neighbor_steps = (1, -1, 8, -8, 7, -7, 9, -9)

def reference(features, stale_features, stale_grads, send_rows, send_count, tile_block, neighbor_slot, labels, w_self, w_neigh, bias, w_cls):
    step_list = jnp.array(neighbor_steps, jnp.int32)
    partitions = jnp.arange(N_DOM, dtype=jnp.int32)
    positions = jnp.arange(CAP, dtype=jnp.int32)
    list_index = jnp.arange(NOFF, dtype=jnp.int32)
    stale_parts = stale_features.reshape(N_DOM, V_DEV, F)
    row_lists = send_rows.reshape(N_DOM, NOFF, CAP)
    live_mask = positions[None, None, :] < send_count[:, :, None]
    packed = jax.vmap(lambda part_rows, index_rows: part_rows[index_rows])(stale_parts, row_lists)
    packed = jnp.where(live_mask[..., None], packed, jnp.zeros((), jnp.bfloat16))
    source = partitions[:, None] - step_list[None, :]
    in_range = (source >= 0) & (source < N_DOM)
    boundary = packed[jnp.clip(source, 0, N_DOM - 1), list_index[None, :]]
    boundary = jnp.where(in_range[:, :, None, None], boundary, jnp.zeros((), jnp.bfloat16))
    extended = jnp.concatenate([features.reshape(N_DOM, V_DEV, F), boundary.reshape(N_DOM, NOFF * CAP, F)], axis=1)
    tiles_all = tile_block.reshape(N_DOM, BLOCKS, TILES)
    slots = neighbor_slot.reshape(N_DOM, BLOCKS, BLOCK, K)
    which_tile = slots // BLOCK
    within = slots % BLOCK
    source_block = jax.vmap(jax.vmap(lambda tile_row, pick: tile_row[pick]))(tiles_all, which_tile)
    ext_index = (source_block * BLOCK + within).reshape(N_DOM, V_DEV * K).astype(jnp.int32)

    def mean_rows(pair):
        ext_rows, index_rows = pair
        picked = ext_rows[index_rows].astype(jnp.float32).reshape(V_DEV, K, F)
        return lax.optimization_barrier(jnp.sum(picked, axis=1)) * (1.0 / K)
    neighbor_mean = lax.map(mean_rows, (extended, ext_index)).reshape(VOXELS, F).astype(jnp.bfloat16)
    preact = jnp.dot(features, w_self, preferred_element_type=jnp.float32) + jnp.dot(neighbor_mean, w_neigh, preferred_element_type=jnp.float32) + bias
    hidden = jax.nn.silu(preact).astype(jnp.bfloat16)
    logits = jnp.dot(hidden, w_cls, preferred_element_type=jnp.float32)
    expo = jnp.exp(logits)
    probs = expo / lax.optimization_barrier(jnp.sum(expo, axis=-1, keepdims=True))
    target_hot = (labels[:, None] == jnp.arange(C, dtype=jnp.int32)[None, :]).astype(jnp.float32)
    dlogits = probs - target_hot
    dhidden = jnp.dot(dlogits, w_cls.astype(jnp.float32).T, precision=lax.Precision.HIGHEST, preferred_element_type=jnp.float32)
    sigma = jax.nn.sigmoid(preact)
    dpre = dhidden * sigma * (1.0 + preact * (1.0 - sigma))
    dpre_b = dpre.astype(jnp.bfloat16)
    scale = 1.0 / math.sqrt(VOXELS)
    grad_w_self = jnp.dot(features.T, dpre_b, preferred_element_type=jnp.float32) * scale
    grad_w_neigh = jnp.dot(neighbor_mean.T, dpre_b, preferred_element_type=jnp.float32) * scale
    grad_bias = lax.optimization_barrier(jnp.sum(dpre, axis=0)) * scale
    grad_w_cls = jnp.dot(hidden.astype(jnp.float32).T, dlogits, precision=lax.Precision.HIGHEST, preferred_element_type=jnp.float32) * scale
    dself = jnp.dot(dpre_b, w_self.T, preferred_element_type=jnp.float32)
    dmean = jnp.dot(dpre_b, w_neigh.T, preferred_element_type=jnp.float32).astype(jnp.bfloat16)

    def spread_rows(pair):
        index_rows, grad_rows = pair
        terms = jnp.repeat(grad_rows.astype(jnp.float32) * (1.0 / K), K, axis=0)
        return jnp.zeros((EXT_BLOCKS * BLOCK, F), jnp.float32).at[index_rows].add(terms)
    dextended = lax.map(spread_rows, (ext_index, dmean.reshape(N_DOM, V_DEV, F)))
    halo_grad = dextended[:, V_DEV:].reshape(HALO, F)
    owner_of = partitions[:, None] + step_list[None, :]
    owner_ok = (owner_of >= 0) & (owner_of < N_DOM)
    grad_parts = stale_grads.reshape(N_DOM, NOFF, CAP, F)
    returned = grad_parts[jnp.clip(owner_of, 0, N_DOM - 1), list_index[None, :]].astype(jnp.float32)
    keep = owner_ok[:, :, None] & live_mask
    returned = jnp.where(keep[..., None], returned, 0.0)

    def add_back(pair):
        index_rows, grad_rows = pair
        return jnp.zeros((V_DEV, F), jnp.float32).at[index_rows.reshape(-1)].add(grad_rows.reshape(-1, F))
    added = lax.map(add_back, (row_lists, returned))
    grad_features = dself + dextended[:, :V_DEV].reshape(VOXELS, F) + added.reshape(VOXELS, F)
    return (grad_features, halo_grad, grad_w_self, grad_w_neigh, grad_bias, grad_w_cls)
```

```python
import functools
import math

import jax
import jax.numpy as jnp
from jax import lax
from jax.experimental import pallas as pl
from jax.experimental.pallas import tpu as pltpu
from jax.sharding import PartitionSpec as P

BLOCK = 128
BF = jnp.bfloat16
F32 = jnp.float32
neighbor_steps = (1, -1, 8, -8, 7, -7, 9, -9)
send_order = (2, 3, 4, 5, 6, 7, 0, 1)
STEP_BLOCKS = 8
SUB = 256


def dot(a, b):
    return jnp.dot(a, b, preferred_element_type=F32)


def exchange_kernel(n, packed, grads, boundary, back, send_sem, recv_sem):
    me = lax.axis_index("dom")

    def valid(index):
        return (index >= 0) & (index < n)

    barrier = pltpu.get_barrier_semaphore()
    expected = 0
    for step in neighbor_steps:
        other = me + step

        @pl.when(valid(other))
        def _():
            pl.semaphore_signal(barrier, inc=1, device_id={"dom": other})

        expected = expected + jnp.where(valid(other), 1, 0)
    pl.semaphore_wait(barrier, expected)

    def copy_of(kind, o, sign):
        src, dst = ((packed, boundary), (grads, back))[kind]
        return pltpu.make_async_remote_copy(
            src_ref=src.at[o],
            dst_ref=dst.at[o],
            send_sem=send_sem.at[kind, o],
            recv_sem=recv_sem.at[kind, o],
            device_id={"dom": me + sign * neighbor_steps[o]},
        )

    for kind, sign in ((0, 1), (1, -1)):
        for o in send_order:

            @pl.when(valid(me + sign * neighbor_steps[o]))
            def _():
                copy_of(kind, o, sign).start()

    for kind, sign in ((0, 1), (1, -1)):
        for o in send_order:
            dst = (boundary, back)[kind]

            @pl.when(jnp.logical_not(valid(me - sign * neighbor_steps[o])))
            def _():
                dst[o] = jnp.zeros(dst.shape[1:], dst.dtype)

    for kind, sign in ((0, 1), (1, -1)):
        for o in send_order:

            @pl.when(valid(me - sign * neighbor_steps[o]))
            def _():
                copy_of(kind, o, sign).wait_recv()

            @pl.when(valid(me + sign * neighbor_steps[o]))
            def _():
                copy_of(kind, o, sign).wait_send()


def exchange(n, packed, grads):
    shape = jax.ShapeDtypeStruct(packed.shape, packed.dtype)
    vmem = pl.BlockSpec(memory_space=pltpu.VMEM)
    return pl.pallas_call(
        functools.partial(exchange_kernel, n),
        out_shape=(shape, shape),
        in_specs=[vmem, vmem],
        out_specs=(vmem, vmem),
        scratch_shapes=[
            pltpu.SemaphoreType.DMA((2, len(neighbor_steps))),
            pltpu.SemaphoreType.DMA((2, len(neighbor_steps))),
        ],
        compiler_params=pltpu.CompilerParams(collective_id=0, has_side_effects=True),
        name="exchange",
    )(packed, grads)


def layer_kernel(
    classes,
    tiles,
    feat,
    bnd,
    back,
    rows,
    slots,
    labels,
    wt,
    bias,
    wct,
    wc2,
    out_g,
    out_h,
    out_w,
    ext_t,
    dext,
    adj,
    xt,
    marks,
    gw,
    gcls,
    gbias,
    sems,
):
    i = pl.program_id(0)
    v_blocks = feat.shape[0] // BLOCK
    b_blocks = bnd.shape[0] // BLOCK
    n_tiles = adj.shape[1] // BLOCK
    k_each = slots.shape[0]

    @pl.when(i == 0)
    def _():
        @pl.loop(0, v_blocks // 8)
        def _(c):
            for u in range(8):
                e = c * 8 + u
                ext_t[e] = feat[pl.ds(pl.multiple_of(e * BLOCK, BLOCK), BLOCK), :].T
                dext[e] = jnp.zeros((BLOCK, BLOCK), F32)

        for u in range(b_blocks):
            ext_t[v_blocks + u] = bnd[u * BLOCK : (u + 1) * BLOCK, :].T
            dext[v_blocks + u] = jnp.zeros((BLOCK, BLOCK), F32)
        gw[...] = jnp.zeros_like(gw)
        gcls[...] = jnp.zeros_like(gcls)
        gbias[...] = jnp.zeros_like(gbias)
        low = rows[...] & (BLOCK - 1)
        high = (rows[...] >> 7).astype(F32)
        within = lax.broadcasted_iota(jnp.int32, marks.shape, 0)
        marks[...] = jnp.where(within == low, high, -1.0).astype(BF)

    row_id = lax.broadcasted_iota(jnp.int32, (BLOCK, BLOCK), 0)
    for j in range(STEP_BLOCKS):
        lanes = slice(j * BLOCK, (j + 1) * BLOCK)
        q = slots[:, lanes]
        low = q & (BLOCK - 1)
        weight = jnp.left_shift(jnp.ones_like(q), (q >> 7) * 4)
        digits = jnp.zeros((BLOCK, BLOCK), jnp.int32)
        for k in range(k_each):
            digits += jnp.where(row_id == low[k : k + 1, :], weight[k : k + 1, :], 0)
        total = jnp.zeros((BLOCK, BLOCK), F32)
        for t in range(n_tiles):
            count = ((digits >> (4 * t)) & 15).astype(F32).astype(BF)
            adj[j, t * BLOCK : (t + 1) * BLOCK, :] = count
        slab = jnp.concatenate(
            [ext_t[tiles[(i * STEP_BLOCKS + j) * n_tiles + t]] for t in range(n_tiles)], axis=1
        )
        total = dot(slab, adj[j])
        xt[:BLOCK, lanes] = ext_t[i * STEP_BLOCKS + j]
        xt[BLOCK:, lanes] = (total * (1.0 / k_each)).astype(BF)

    class_id = lax.broadcasted_iota(jnp.int32, (wct.shape[0], SUB), 0)
    dmeans = []
    for s in range(STEP_BLOCKS * BLOCK // SUB):
        lanes = slice(s * SUB, (s + 1) * SUB)
        x = xt[:, lanes]
        pre = dot(wt[...], x) + bias[...]
        sigma = 1.0 / (1.0 + jnp.exp(-pre))
        hidden = (pre * sigma).astype(BF)
        slope = sigma * (1.0 + pre * (1.0 - sigma))
        logits = dot(wct[...], hidden)
        expo = jnp.where(class_id < classes, jnp.exp(logits), 0.0)
        probs = expo / jnp.sum(expo, axis=0, keepdims=True)
        dlog = probs - jnp.where(class_id == labels[:, lanes], 1.0, 0.0)
        d_hi = dlog.astype(BF)
        d_lo = (dlog - d_hi.astype(F32)).astype(BF)
        d2 = jnp.concatenate([d_hi, d_lo], axis=0)
        dpre = dot(wc2[...], d2) * slope
        gbias[...] += dpre[:, :BLOCK] + dpre[:, BLOCK:]
        dpb = dpre.astype(BF).T
        gcls[...] += dot(hidden, d2.T)
        gw[...] += dot(x, dpb)
        both = dot(dpb, wt[...])
        dmeans.append((both[:, BLOCK:].astype(BF) * BF(1.0 / k_each)))
        for u in range(SUB // BLOCK):
            b = i * STEP_BLOCKS + s * (SUB // BLOCK) + u
            spread = jnp.where(
                marks[...] == (jnp.zeros((1, 1), jnp.int32) + b).astype(F32).astype(BF), BF(1), BF(0)
            )
            dext[b] += both[u * BLOCK : (u + 1) * BLOCK, :BLOCK] + dot(spread, back[...])

    for j in range(STEP_BLOCKS):
        part = dmeans[j * BLOCK // SUB]
        at = j * BLOCK % SUB
        dslab = dot(adj[j], part[at : at + BLOCK, :])
        for t in range(n_tiles):
            e = tiles[(i * STEP_BLOCKS + j) * n_tiles + t]
            dext[e] += dslab[t * BLOCK : (t + 1) * BLOCK, :]

    @pl.when(i == pl.num_programs(0) - 1)
    def _():
        own = pltpu.make_async_copy(dext.at[pl.ds(0, v_blocks)], out_g, sems.at[0])
        halo = pltpu.make_async_copy(dext.at[pl.ds(v_blocks, b_blocks)], out_h, sems.at[1])
        own.start()
        halo.start()
        n_w = gw.shape[0]
        half = gcls.shape[1] // 2
        by_class = gcls[...].T
        out_w[:n_w, :] = gw[...]
        out_w[n_w : n_w + half, :] = by_class[:half, :] + by_class[half:, :]
        out_w[n_w + half : n_w + half + 8, :] = jnp.broadcast_to(
            jnp.sum(gbias[...].T, axis=0, keepdims=True), (8, BLOCK)
        )
        out_w[n_w + half + 8 :, :] = jnp.zeros((out_w.shape[0] - n_w - half - 8, BLOCK), F32)
        own.wait()
        halo.wait()


def layer(n, features, boundary, back, rows, tiles, slots, labels, wt, bias, wct, wc2, classes):
    v_dev, width = features.shape
    v_blocks = v_dev // BLOCK
    b_blocks = boundary.shape[0] // BLOCK
    n_tiles = tiles.shape[0] // v_blocks
    grid = v_blocks // STEP_BLOCKS
    chunk = STEP_BLOCKS * BLOCK
    used = 2 * width + wct.shape[0] + 8
    unit = 8 * n
    w_rows = -(-used // unit) * unit

    def whole(array):
        return pl.BlockSpec(array.shape, lambda i: (0,) * array.ndim)

    return pl.pallas_call(
        functools.partial(layer_kernel, classes),
        grid=(grid,),
        out_shape=(
            jax.ShapeDtypeStruct((v_blocks, BLOCK, width), F32),
            jax.ShapeDtypeStruct((b_blocks, BLOCK, width), F32),
            jax.ShapeDtypeStruct((w_rows, width), F32),
        ),
        in_specs=[
            pl.BlockSpec(memory_space=pltpu.SMEM),
            whole(features),
            whole(boundary),
            whole(back),
            whole(rows),
            pl.BlockSpec((slots.shape[0], chunk), lambda i: (0, i)),
            pl.BlockSpec((1, chunk), lambda i: (0, i)),
            whole(wt),
            whole(bias),
            whole(wct),
            whole(wc2),
        ],
        out_specs=(
            pl.BlockSpec(memory_space=pl.ANY),
            pl.BlockSpec(memory_space=pl.ANY),
            pl.BlockSpec((w_rows, width), lambda i: (0, 0)),
        ),
        scratch_shapes=[
            pltpu.VMEM((v_blocks + b_blocks, width, BLOCK), BF),
            pltpu.VMEM((v_blocks + b_blocks, BLOCK, width), F32),
            pltpu.VMEM((STEP_BLOCKS, n_tiles * BLOCK, BLOCK), BF),
            pltpu.VMEM((2 * width, chunk), BF),
            pltpu.VMEM((BLOCK, rows.shape[1]), BF),
            pltpu.VMEM((2 * width, width), F32),
            pltpu.VMEM((width, 2 * wct.shape[0]), F32),
            pltpu.VMEM((width, BLOCK), F32),
            pltpu.SemaphoreType.DMA((2,)),
        ],
        compiler_params=pltpu.CompilerParams(
            dimension_semantics=("arbitrary",), vmem_limit_bytes=48 * 1024 * 1024
        ),
        name="layer",
    )(tiles, features, boundary, back, rows, slots, labels, wt, bias, wct, wc2)


def reduce_kernel(n, near, scale, src, out, buf1, buf2, acc, mine, sem):
    me = lax.axis_index("dom")
    far = n // near
    a = lax.rem(me, near)
    z = lax.div(me, near)
    wide = src.shape[0] // near
    narrow = wide // far

    def near_id(d):
        return lax.rem(a + d, near)

    def far_id(d):
        return lax.rem(z + d, far)

    barrier = pltpu.get_barrier_semaphore()
    for d in range(1, near):
        pl.semaphore_signal(barrier, inc=1, device_id={"dom": z * near + near_id(d)})
    for d in range(1, far):
        pl.semaphore_signal(barrier, inc=1, device_id={"dom": far_id(d) * near + a})
    pl.semaphore_wait(barrier, near + far - 2)

    def rows(start, size):
        return pl.ds(pl.multiple_of(start, 8), size)

    def send(src_ref, dst_ref, slot, device):
        return pltpu.make_async_remote_copy(
            src_ref=src_ref,
            dst_ref=dst_ref,
            send_sem=sem.at[0, slot],
            recv_sem=sem.at[1, slot],
            device_id={"dom": device},
        )

    def run(copies):
        for c in copies:
            c.start()
        for c in copies:
            c.wait()

    run(
        [
            send(src.at[rows(near_id(d) * wide, wide)], buf1.at[d - 1], d - 1, z * near + near_id(d))
            for d in range(1, near)
        ]
    )
    part = src[rows(a * wide, wide), :]
    for d in range(1, near):
        part += buf1[d - 1]
    acc[...] = part
    base = near - 1
    run(
        [
            send(
                acc.at[rows(far_id(d) * narrow, narrow)],
                buf2.at[d - 1],
                base + d - 1,
                far_id(d) * near + a,
            )
            for d in range(1, far)
        ]
    )
    part = acc[rows(z * narrow, narrow), :]
    for d in range(1, far):
        part += buf2[d - 1]
    own = rows(a * wide + z * narrow, narrow)
    mine[...] = part * scale
    out[own, :] = part * scale
    base += far - 1
    run(
        [
            send(mine, out.at[own], base + d - 1, far_id(d) * near + a)
            for d in range(1, far)
        ]
    )
    base += far - 1
    full = rows(a * wide, wide)
    run(
        [
            send(out.at[full], out.at[full], base + d - 1, z * near + near_id(d))
            for d in range(1, near)
        ]
    )


def reduce_all(n, partial, scale):
    near = 4 if n % 4 == 0 else n
    far = n // near
    wide = partial.shape[0] // near
    width = partial.shape[1]
    vmem = pl.BlockSpec(memory_space=pltpu.VMEM)
    return pl.pallas_call(
        functools.partial(reduce_kernel, n, near, scale),
        out_shape=jax.ShapeDtypeStruct(partial.shape, F32),
        in_specs=[vmem],
        out_specs=vmem,
        scratch_shapes=[
            pltpu.VMEM((near - 1, wide, width), F32),
            pltpu.VMEM((max(far - 1, 1), wide // far, width), F32),
            pltpu.VMEM((wide, width), F32),
            pltpu.VMEM((wide // far, width), F32),
            pltpu.SemaphoreType.DMA((2, 2 * (near + far - 2))),
        ],
        compiler_params=pltpu.CompilerParams(collective_id=1, has_side_effects=True),
        name="reduce",
    )(partial)


def run_layer_raw(
    n, features, boundary, back, rows, tb, slots, labels, w_self, w_neigh, bias, w_cls
):
    classes = w_cls.shape[1]
    wt = jnp.concatenate([w_self.T, w_neigh.T], axis=1)
    wct = jnp.pad(w_cls.T, ((0, 16 - classes), (0, 0)))
    wc = jnp.pad(w_cls, ((0, 0), (0, 16 - classes)))
    wc2 = jnp.concatenate([wc, wc], axis=1)
    return layer(
        n,
        features,
        boundary,
        back,
        rows.reshape(1, -1),
        tb.reshape(-1),
        slots.T,
        labels.reshape(1, -1),
        wt,
        bias.reshape(-1, 1),
        wct,
        wc2,
        classes,
    )


def run_layer(n, *args):
    width = args[0].shape[1]
    classes = args[-1].shape[1]
    grad, halo, total = run_layer_raw(n, *args)
    return (
        grad.reshape(-1, width),
        halo.reshape(-1, width),
        total[:width],
        total[width : 2 * width],
        total[2 * width + 16],
        total[2 * width : 2 * width + classes].T,
    )


def body(
    n,
    features,
    stale_features,
    stale_grads,
    send_rows,
    send_count,
    tile_block,
    neighbor_slot,
    labels,
    w_self,
    w_neigh,
    bias,
    w_cls,
):
    v_dev, width = features.shape
    classes = w_cls.shape[1]
    positions = jnp.arange(send_rows.shape[1], dtype=jnp.int32)
    live = positions[None, :] < send_count[0][:, None]
    packed = jnp.where(live[:, :, None], stale_features[send_rows], jnp.zeros((), BF))
    boundary, back = exchange(n, packed, stale_grads.reshape(packed.shape))
    grad, halo, partial = run_layer_raw(
        n,
        features,
        boundary.reshape(-1, width),
        back.reshape(-1, width),
        jnp.where(live, send_rows, -1),
        tile_block,
        neighbor_slot,
        labels,
        w_self,
        w_neigh,
        bias,
        w_cls,
    )
    scale = 1.0 / math.sqrt(v_dev * n)
    total = reduce_all(n, partial, scale)
    return (
        grad.reshape(v_dev, width),
        halo.reshape(-1, width),
        total[:width],
        total[width : 2 * width],
        total[2 * width + 16],
        total[2 * width : 2 * width + classes].T,
    )


def solution(mesh):
    split = P(("groups", "dom"), None)
    placed = (split,) * 7 + (P(("groups", "dom")),) + (P(),) * 4
    return jax.shard_map(
        functools.partial(body, mesh.shape["dom"]),
        mesh=mesh,
        in_specs=placed,
        out_specs=(
            split,
            split,
            P("groups", None),
            P("groups", None),
            P("groups"),
            P("groups", None),
        ),
        check_vma=False,
    )
```

```python
import functools
import math

import jax
import jax.numpy as jnp
from jax import lax
from jax.experimental import pallas as pl
from jax.experimental.pallas import tpu as pltpu
from jax.sharding import PartitionSpec as P

BLOCK = 128
BF = jnp.bfloat16
F32 = jnp.float32
neighbor_steps = (1, -1, 8, -8, 7, -7, 9, -9)
send_order = (2, 3, 4, 5, 6, 7, 0, 1)
STEP_BLOCKS = 8
SUB = 256


def dot(a, b):
    return jnp.dot(a, b, preferred_element_type=F32)


def exchange_kernel(
    n, count, rows, stale, grads, boundary, back, masked, packed, marks, send_sem, recv_sem
):
    me = lax.axis_index("dom")
    lists, cap = rows.shape
    chunk = 8
    group = 2

    def valid(index):
        return (index >= 0) & (index < n)

    barrier = pltpu.get_barrier_semaphore()
    expected = 0
    for step in neighbor_steps:
        other = me + step

        @pl.when(valid(other))
        def _():
            pl.semaphore_signal(barrier, inc=1, device_id={"dom": other})

        expected = expected + jnp.where(valid(other), 1, 0)

    def copy_of(kind, o, sign):
        src, dst = ((packed, boundary), (grads, back))[kind]
        return pltpu.make_async_remote_copy(
            src_ref=src.at[o],
            dst_ref=dst.at[o],
            send_sem=send_sem.at[kind, o],
            recv_sem=recv_sem.at[kind, o],
            device_id={"dom": me + sign * neighbor_steps[o]},
        )

    def start(kind, o, sign):
        @pl.when(valid(me + sign * neighbor_steps[o]))
        def _():
            copy_of(kind, o, sign).start()

    place = lax.broadcasted_iota(jnp.int32, (1, cap), 1)
    for o in range(lists):
        masked[o : o + 1, :] = jnp.where(place < count[0, o], rows[o : o + 1, :], -1)
    listed = masked[...]
    low = (listed & (BLOCK - 1)).astype(F32)
    high = (listed >> 7).astype(F32)
    pad = jnp.zeros((cap - lists, cap), F32)
    low = jnp.concatenate([low, pad], axis=0).T
    high = jnp.concatenate([high, pad], axis=0).T
    lane = lax.broadcasted_iota(jnp.int32, (cap, BLOCK), 1).astype(F32)
    for o in range(lists):
        marks[o * cap : (o + 1) * cap, :] = jnp.where(
            low[:, o : o + 1] == lane, high[:, o : o + 1], -1.0
        ).astype(BF)

    pl.semaphore_wait(barrier, expected)
    for o in send_order:
        start(1, o, -1)

    for g in range(0, lists, group):
        listed_at = [send_order[g + u] for u in range(group)]
        mark = jnp.concatenate([marks[o * cap : (o + 1) * cap, :] for o in listed_at], axis=0)

        def some(c, acc):
            hot = jnp.concatenate(
                [
                    jnp.where(mark == (c * chunk + u).astype(F32).astype(BF), BF(1), BF(0))
                    for u in range(chunk)
                ],
                axis=1,
            )
            at = pl.multiple_of(c * chunk * BLOCK, chunk * BLOCK)
            return acc + dot(hot, stale[pl.ds(at, chunk * BLOCK), :])

        acc = lax.fori_loop(
            0,
            stale.shape[0] // (chunk * BLOCK),
            some,
            jnp.zeros((group * cap, stale.shape[1]), F32),
        )
        for u, o in enumerate(listed_at):
            packed[o] = acc[u * cap : (u + 1) * cap, :].astype(BF)
            start(0, o, 1)

    for kind, sign in ((0, 1), (1, -1)):
        for o in send_order:
            dst = (boundary, back)[kind]

            @pl.when(jnp.logical_not(valid(me - sign * neighbor_steps[o])))
            def _():
                dst[o] = jnp.zeros(dst.shape[1:], dst.dtype)

    for kind, sign in ((1, -1), (0, 1)):
        for o in send_order:

            @pl.when(valid(me - sign * neighbor_steps[o]))
            def _():
                copy_of(kind, o, sign).wait_recv()

            @pl.when(valid(me + sign * neighbor_steps[o]))
            def _():
                copy_of(kind, o, sign).wait_send()


def exchange(n, count, rows, stale, grads):
    lists, cap = rows.shape
    width = stale.shape[1]
    shape = jax.ShapeDtypeStruct((lists, cap, width), BF)
    vmem = pl.BlockSpec(memory_space=pltpu.VMEM)
    return pl.pallas_call(
        functools.partial(exchange_kernel, n),
        out_shape=(shape, shape, jax.ShapeDtypeStruct(rows.shape, jnp.int32)),
        in_specs=[pl.BlockSpec(memory_space=pltpu.SMEM), vmem, vmem, vmem],
        out_specs=(vmem, vmem, vmem),
        scratch_shapes=[
            pltpu.VMEM((lists, cap, width), BF),
            pltpu.VMEM((lists * cap, BLOCK), BF),
            pltpu.SemaphoreType.DMA((2, lists)),
            pltpu.SemaphoreType.DMA((2, lists)),
        ],
        compiler_params=pltpu.CompilerParams(
            collective_id=0, has_side_effects=True, vmem_limit_bytes=40 * 1024 * 1024
        ),
        name="exchange",
    )(count, rows, stale, grads)


def layer_kernel(
    classes,
    tiles,
    feat,
    bnd,
    back,
    rows,
    slots,
    labels,
    w_self,
    w_neigh,
    bias_row,
    wct_raw,
    out_g,
    out_h,
    out_w,
    ext_t,
    dext,
    adj,
    xt,
    marks,
    gw,
    gcls,
    gbias,
    wt,
    wct,
    wc2,
    bias,
    sems,
):
    i = pl.program_id(0)
    v_blocks = feat.shape[0] // BLOCK
    b_blocks = bnd.shape[0] // BLOCK
    n_tiles = adj.shape[1] // BLOCK
    k_each = slots.shape[0]

    @pl.when(i == 0)
    def _():
        @pl.loop(0, v_blocks // 8)
        def _(c):
            for u in range(8):
                e = c * 8 + u
                ext_t[e] = feat[pl.ds(pl.multiple_of(e * BLOCK, BLOCK), BLOCK), :].T
                dext[e] = jnp.zeros((BLOCK, BLOCK), F32)

        for u in range(b_blocks):
            ext_t[v_blocks + u] = bnd[u * BLOCK : (u + 1) * BLOCK, :].T
            dext[v_blocks + u] = jnp.zeros((BLOCK, BLOCK), F32)
        gw[...] = jnp.zeros_like(gw)
        wt[:, :BLOCK] = w_self[...].T
        wt[:, BLOCK:] = w_neigh[...].T
        used = wct_raw.shape[0]
        padded = jnp.concatenate(
            [wct_raw[...].astype(F32), jnp.zeros((BLOCK - used, BLOCK), F32)], axis=0
        )
        half = wct.shape[0]
        wct[...] = padded[:half, :].astype(BF)
        side = padded.T[:, :half].astype(BF)
        wc2[:, :half] = side
        wc2[:, half:] = side
        bias[...] = jnp.broadcast_to(bias_row[...], (BLOCK, BLOCK)).T
        gcls[...] = jnp.zeros_like(gcls)
        gbias[...] = jnp.zeros_like(gbias)
        low = rows[...] & (BLOCK - 1)
        high = (rows[...] >> 7).astype(F32)
        within = lax.broadcasted_iota(jnp.int32, marks.shape, 0)
        marks[...] = jnp.where(within == low, high, -1.0).astype(BF)

    row_id = lax.broadcasted_iota(jnp.int32, (BLOCK, BLOCK), 0)
    for j in range(STEP_BLOCKS):
        lanes = slice(j * BLOCK, (j + 1) * BLOCK)
        q = slots[:, lanes]
        low = q & (BLOCK - 1)
        weight = jnp.left_shift(jnp.ones_like(q), (q >> 7) * 4)
        digits = jnp.zeros((BLOCK, BLOCK), jnp.int32)
        for k in range(k_each):
            digits += jnp.where(row_id == low[k : k + 1, :], weight[k : k + 1, :], 0)
        total = jnp.zeros((BLOCK, BLOCK), F32)
        for t in range(n_tiles):
            count = ((digits >> (4 * t)) & 15).astype(F32).astype(BF)
            adj[j, t * BLOCK : (t + 1) * BLOCK, :] = count
        slab = jnp.concatenate(
            [ext_t[tiles[t, i * STEP_BLOCKS + j]] for t in range(n_tiles)], axis=1
        )
        total = dot(slab, adj[j])
        xt[:BLOCK, lanes] = ext_t[i * STEP_BLOCKS + j]
        xt[BLOCK:, lanes] = (total * (1.0 / k_each)).astype(BF)

    class_id = lax.broadcasted_iota(jnp.int32, (wct.shape[0], SUB), 0)
    dmeans = []
    for s in range(STEP_BLOCKS * BLOCK // SUB):
        lanes = slice(s * SUB, (s + 1) * SUB)
        x = xt[:, lanes]
        pre = dot(wt[...], x) + jnp.concatenate([bias[...]] * (SUB // BLOCK), axis=1)
        sigma = 1.0 / (1.0 + jnp.exp(-pre))
        hidden = (pre * sigma).astype(BF)
        slope = sigma * (1.0 + pre * (1.0 - sigma))
        logits = dot(wct[...], hidden)
        expo = jnp.where(class_id < classes, jnp.exp(logits), 0.0)
        probs = expo / jnp.sum(expo, axis=0, keepdims=True)
        dlog = probs - jnp.where(class_id == labels[:, lanes], 1.0, 0.0)
        d_hi = dlog.astype(BF)
        d_lo = (dlog - d_hi.astype(F32)).astype(BF)
        d2 = jnp.concatenate([d_hi, d_lo], axis=0)
        dpre = dot(wc2[...], d2) * slope
        gbias[...] += dpre[:, :BLOCK] + dpre[:, BLOCK:]
        dpb = dpre.astype(BF).T
        gcls[...] += dot(hidden, d2.T)
        gw[...] += dot(x, dpb)
        both = dot(dpb, wt[...])
        dmeans.append((both[:, BLOCK:].astype(BF) * BF(1.0 / k_each)))
        for u in range(SUB // BLOCK):
            b = i * STEP_BLOCKS + s * (SUB // BLOCK) + u
            spread = jnp.where(
                marks[...] == (jnp.zeros((1, 1), jnp.int32) + b).astype(F32).astype(BF), BF(1), BF(0)
            )
            dext[b] += both[u * BLOCK : (u + 1) * BLOCK, :BLOCK] + dot(spread, back[...])

    for j in range(STEP_BLOCKS):
        part = dmeans[j * BLOCK // SUB]
        at = j * BLOCK % SUB
        dslab = dot(adj[j], part[at : at + BLOCK, :])
        for t in range(n_tiles):
            e = tiles[t, i * STEP_BLOCKS + j]
            dext[e] += dslab[t * BLOCK : (t + 1) * BLOCK, :]

    @pl.when(i == pl.num_programs(0) - 1)
    def _():
        own = pltpu.make_async_copy(dext.at[pl.ds(0, v_blocks)], out_g, sems.at[0])
        halo = pltpu.make_async_copy(dext.at[pl.ds(v_blocks, b_blocks)], out_h, sems.at[1])
        own.start()
        halo.start()
        n_w = gw.shape[0]
        half = gcls.shape[1] // 2
        by_class = gcls[...].T
        out_w[:n_w, :] = gw[...]
        out_w[n_w : n_w + half, :] = by_class[:half, :] + by_class[half:, :]
        out_w[n_w + half : n_w + half + 8, :] = jnp.broadcast_to(
            jnp.sum(gbias[...].T, axis=0, keepdims=True), (8, BLOCK)
        )
        out_w[n_w + half + 8 :, :] = jnp.zeros((out_w.shape[0] - n_w - half - 8, BLOCK), F32)
        own.wait()
        halo.wait()


def layer(n, features, boundary, back, rows, tiles, slots, labels, w_self, w_neigh, bias, wct):
    v_dev, width = features.shape
    v_blocks = v_dev // BLOCK
    b_blocks = boundary.shape[0] // BLOCK
    n_tiles = tiles.shape[0]
    classes = wct.shape[0]
    half = -(-classes // 16) * 16
    grid = v_blocks // STEP_BLOCKS
    chunk = STEP_BLOCKS * BLOCK
    used = 2 * width + half + 8
    unit = 8 * n
    w_rows = -(-used // unit) * unit

    def whole(array):
        return pl.BlockSpec(array.shape, lambda i: (0,) * array.ndim)

    return pl.pallas_call(
        functools.partial(layer_kernel, classes),
        grid=(grid,),
        out_shape=(
            jax.ShapeDtypeStruct((v_blocks, BLOCK, width), F32),
            jax.ShapeDtypeStruct((b_blocks, BLOCK, width), F32),
            jax.ShapeDtypeStruct((w_rows, width), F32),
        ),
        in_specs=[
            pl.BlockSpec(memory_space=pltpu.SMEM),
            whole(features),
            whole(boundary),
            whole(back),
            whole(rows),
            pl.BlockSpec((slots.shape[0], chunk), lambda i: (0, i)),
            pl.BlockSpec((1, chunk), lambda i: (0, i)),
            whole(w_self),
            whole(w_neigh),
            whole(bias),
            whole(wct),
        ],
        out_specs=(
            pl.BlockSpec(memory_space=pl.ANY),
            pl.BlockSpec(memory_space=pl.ANY),
            pl.BlockSpec((w_rows, width), lambda i: (0, 0)),
        ),
        scratch_shapes=[
            pltpu.VMEM((v_blocks + b_blocks, width, BLOCK), BF),
            pltpu.VMEM((v_blocks + b_blocks, BLOCK, width), F32),
            pltpu.VMEM((STEP_BLOCKS, n_tiles * BLOCK, BLOCK), BF),
            pltpu.VMEM((2 * width, chunk), BF),
            pltpu.VMEM((BLOCK, rows.shape[1]), BF),
            pltpu.VMEM((2 * width, width), F32),
            pltpu.VMEM((width, 2 * half), F32),
            pltpu.VMEM((width, BLOCK), F32),
            pltpu.VMEM((width, 2 * width), BF),
            pltpu.VMEM((half, width), BF),
            pltpu.VMEM((width, 2 * half), BF),
            pltpu.VMEM((width, BLOCK), F32),
            pltpu.SemaphoreType.DMA((2,)),
        ],
        compiler_params=pltpu.CompilerParams(
            dimension_semantics=("arbitrary",), vmem_limit_bytes=48 * 1024 * 1024
        ),
        name="layer",
    )(tiles, features, boundary, back, rows, slots, labels, w_self, w_neigh, bias, wct)


def reduce_kernel(n, near, scale, src, out, buf1, buf2, acc, mine, sem):
    me = lax.axis_index("dom")
    far = n // near
    a = lax.rem(me, near)
    z = lax.div(me, near)
    wide = src.shape[0] // near
    narrow = wide // far

    def near_id(d):
        return lax.rem(a + d, near)

    def far_id(d):
        return lax.rem(z + d, far)

    barrier = pltpu.get_barrier_semaphore()
    for d in range(1, near):
        pl.semaphore_signal(barrier, inc=1, device_id={"dom": z * near + near_id(d)})
    for d in range(1, far):
        pl.semaphore_signal(barrier, inc=1, device_id={"dom": far_id(d) * near + a})
    pl.semaphore_wait(barrier, near + far - 2)

    def rows(start, size):
        return pl.ds(pl.multiple_of(start, 8), size)

    def send(src_ref, dst_ref, slot, device):
        return pltpu.make_async_remote_copy(
            src_ref=src_ref,
            dst_ref=dst_ref,
            send_sem=sem.at[0, slot],
            recv_sem=sem.at[1, slot],
            device_id={"dom": device},
        )

    def run(copies):
        for c in copies:
            c.start()
        for c in copies:
            c.wait()

    run(
        [
            send(src.at[rows(near_id(d) * wide, wide)], buf1.at[d - 1], d - 1, z * near + near_id(d))
            for d in range(1, near)
        ]
    )
    part = src[rows(a * wide, wide), :]
    for d in range(1, near):
        part += buf1[d - 1]
    acc[...] = part
    base = near - 1
    run(
        [
            send(
                acc.at[rows(far_id(d) * narrow, narrow)],
                buf2.at[d - 1],
                base + d - 1,
                far_id(d) * near + a,
            )
            for d in range(1, far)
        ]
    )
    part = acc[rows(z * narrow, narrow), :]
    for d in range(1, far):
        part += buf2[d - 1]
    own = rows(a * wide + z * narrow, narrow)
    mine[...] = part * scale
    out[own, :] = part * scale
    base += far - 1
    run(
        [
            send(mine, out.at[own], base + d - 1, far_id(d) * near + a)
            for d in range(1, far)
        ]
    )
    base += far - 1
    full = rows(a * wide, wide)
    run(
        [
            send(out.at[full], out.at[full], base + d - 1, z * near + near_id(d))
            for d in range(1, near)
        ]
    )


def reduce_all(n, partial, scale):
    near = 4 if n % 4 == 0 else n
    far = n // near
    wide = partial.shape[0] // near
    width = partial.shape[1]
    vmem = pl.BlockSpec(memory_space=pltpu.VMEM)
    return pl.pallas_call(
        functools.partial(reduce_kernel, n, near, scale),
        out_shape=jax.ShapeDtypeStruct(partial.shape, F32),
        in_specs=[vmem],
        out_specs=vmem,
        scratch_shapes=[
            pltpu.VMEM((near - 1, wide, width), F32),
            pltpu.VMEM((max(far - 1, 1), wide // far, width), F32),
            pltpu.VMEM((wide, width), F32),
            pltpu.VMEM((wide // far, width), F32),
            pltpu.SemaphoreType.DMA((2, 2 * (near + far - 2))),
        ],
        compiler_params=pltpu.CompilerParams(collective_id=1, has_side_effects=True),
        name="reduce",
    )(partial)


def run_layer_raw(
    n, features, boundary, back, rows, tb, slots, labels, w_self, w_neigh, bias, w_cls
):
    return layer(
        n,
        features,
        boundary,
        back,
        rows.reshape(1, -1),
        tb.T,
        slots.T,
        labels.reshape(1, -1),
        w_self,
        w_neigh,
        bias.reshape(1, -1),
        w_cls.T,
    )


def run_layer(n, *args):
    width = args[0].shape[1]
    classes = args[-1].shape[1]
    grad, halo, total = run_layer_raw(n, *args)
    return (
        grad.reshape(-1, width),
        halo.reshape(-1, width),
        total[:width],
        total[width : 2 * width],
        total[2 * width + 16],
        total[2 * width : 2 * width + classes].T,
    )


def body(
    n,
    features,
    stale_features,
    stale_grads,
    send_rows,
    send_count,
    tile_block,
    neighbor_slot,
    labels,
    w_self,
    w_neigh,
    bias,
    w_cls,
):
    v_dev, width = features.shape
    classes = w_cls.shape[1]
    boundary, back, rows = exchange(
        n, send_count, send_rows, stale_features, stale_grads.reshape(send_rows.shape + (width,))
    )
    grad, halo, partial = run_layer_raw(
        n,
        features,
        boundary.reshape(-1, width),
        back.reshape(-1, width),
        rows,
        tile_block,
        neighbor_slot,
        labels,
        w_self,
        w_neigh,
        bias,
        w_cls,
    )
    scale = 1.0 / math.sqrt(v_dev * n)
    total = reduce_all(n, partial, scale)
    return (
        grad.reshape(v_dev, width),
        halo.reshape(-1, width),
        total[:width],
        total[width : 2 * width],
        total[2 * width + 16],
        total[2 * width : 2 * width + classes].T,
    )


def solution(mesh):
    split = P(("groups", "dom"), None)
    placed = (split,) * 7 + (P(("groups", "dom")),) + (P(),) * 4
    return jax.shard_map(
        functools.partial(body, mesh.shape["dom"]),
        mesh=mesh,
        in_specs=placed,
        out_specs=(
            split,
            split,
            P("groups", None),
            P("groups", None),
            P("groups"),
            P("groups", None),
        ),
        check_vma=False,
    )
```

```python
import functools
import math

import jax
import jax.numpy as jnp
from jax import lax
from jax.experimental import pallas as pl
from jax.experimental.pallas import tpu as pltpu
from jax.sharding import PartitionSpec as P

BLOCK = 128
BF = jnp.bfloat16
F32 = jnp.float32
neighbor_steps = (1, -1, 8, -8, 7, -7, 9, -9)
send_order = (2, 3, 4, 5, 6, 7, 0, 1)
STEP_BLOCKS = 8
SUB = 256


def dot(a, b):
    return jnp.dot(a, b, preferred_element_type=F32)


def exchange_kernel(
    n, count, rows, stale_hbm, grads, boundary, back, masked, packed, marks, stale, send_sem, recv_sem, sem
):
    me = lax.axis_index("dom")
    lists, cap = rows.shape
    chunk = 8
    group = 2

    def valid(index):
        return (index >= 0) & (index < n)

    fetch = pltpu.make_async_copy(stale_hbm, stale, sem)
    fetch.start()
    barrier = pltpu.get_barrier_semaphore()
    expected = 0
    for step in neighbor_steps:
        other = me + step

        @pl.when(valid(other))
        def _():
            pl.semaphore_signal(barrier, inc=1, device_id={"dom": other})

        expected = expected + jnp.where(valid(other), 1, 0)

    def copy_of(kind, o, sign):
        src, dst = ((packed, boundary), (grads, back))[kind]
        return pltpu.make_async_remote_copy(
            src_ref=src.at[o],
            dst_ref=dst.at[o],
            send_sem=send_sem.at[kind, o],
            recv_sem=recv_sem.at[kind, o],
            device_id={"dom": me + sign * neighbor_steps[o]},
        )

    def start(kind, o, sign):
        @pl.when(valid(me + sign * neighbor_steps[o]))
        def _():
            copy_of(kind, o, sign).start()

    place = lax.broadcasted_iota(jnp.int32, (1, cap), 1)
    for o in range(lists):
        masked[o : o + 1, :] = jnp.where(place < count[0, o], rows[o : o + 1, :], -1)
    listed = masked[...]
    low = (listed & (BLOCK - 1)).astype(F32)
    high = (listed >> 7).astype(F32)
    pad = jnp.zeros((cap - lists, cap), F32)
    low = jnp.concatenate([low, pad], axis=0).T
    high = jnp.concatenate([high, pad], axis=0).T
    lane = lax.broadcasted_iota(jnp.int32, (cap, BLOCK), 1).astype(F32)
    for o in range(lists):
        marks[o * cap : (o + 1) * cap, :] = jnp.where(
            low[:, o : o + 1] == lane, high[:, o : o + 1], -1.0
        ).astype(BF)

    pl.semaphore_wait(barrier, expected)
    for o in send_order:
        start(1, o, -1)

    fetch.wait()
    for g in range(0, lists, group):
        listed_at = [send_order[g + u] for u in range(group)]
        mark = jnp.concatenate([marks[o * cap : (o + 1) * cap, :] for o in listed_at], axis=0)

        def some(c, acc):
            hot = jnp.concatenate(
                [
                    jnp.where(mark == (c * chunk + u).astype(F32).astype(BF), BF(1), BF(0))
                    for u in range(chunk)
                ],
                axis=1,
            )
            at = pl.multiple_of(c * chunk * BLOCK, chunk * BLOCK)
            return acc + dot(hot, stale[pl.ds(at, chunk * BLOCK), :])

        acc = lax.fori_loop(
            0,
            stale.shape[0] // (chunk * BLOCK),
            some,
            jnp.zeros((group * cap, stale.shape[1]), F32),
        )
        for u, o in enumerate(listed_at):
            packed[o] = acc[u * cap : (u + 1) * cap, :].astype(BF)
            start(0, o, 1)

    for kind, sign in ((0, 1), (1, -1)):
        for o in send_order:
            dst = (boundary, back)[kind]

            @pl.when(jnp.logical_not(valid(me - sign * neighbor_steps[o])))
            def _():
                dst[o] = jnp.zeros(dst.shape[1:], dst.dtype)

    for kind, sign in ((1, -1), (0, 1)):
        for o in send_order:

            @pl.when(valid(me - sign * neighbor_steps[o]))
            def _():
                copy_of(kind, o, sign).wait_recv()

            @pl.when(valid(me + sign * neighbor_steps[o]))
            def _():
                copy_of(kind, o, sign).wait_send()


def exchange(n, count, rows, stale, grads):
    lists, cap = rows.shape
    width = stale.shape[1]
    shape = jax.ShapeDtypeStruct((lists, cap, width), BF)
    vmem = pl.BlockSpec(memory_space=pltpu.VMEM)
    hbm = pl.BlockSpec(memory_space=pl.ANY)
    return pl.pallas_call(
        functools.partial(exchange_kernel, n),
        out_shape=(shape, shape, jax.ShapeDtypeStruct(rows.shape, jnp.int32)),
        in_specs=[pl.BlockSpec(memory_space=pltpu.SMEM), vmem, hbm, hbm],
        out_specs=(vmem, vmem, vmem),
        scratch_shapes=[
            pltpu.VMEM((lists, cap, width), BF),
            pltpu.VMEM((lists * cap, BLOCK), BF),
            pltpu.VMEM(stale.shape, BF),
            pltpu.SemaphoreType.DMA((2, lists)),
            pltpu.SemaphoreType.DMA((2, lists)),
            pltpu.SemaphoreType.DMA,
        ],
        compiler_params=pltpu.CompilerParams(
            collective_id=0, has_side_effects=True, vmem_limit_bytes=58 * 1024 * 1024
        ),
        name="exchange",
    )(count, rows, stale, grads)


def layer_kernel(
    classes,
    tiles,
    feat,
    bnd,
    back,
    rows,
    slots,
    labels,
    w_self_hbm,
    w_neigh_hbm,
    bias_row,
    wct_raw,
    out_g,
    out_h,
    out_w,
    ext_t,
    dext,
    adj,
    xt,
    marks,
    gw,
    gcls,
    gbias,
    wt,
    wct,
    wc2,
    bias,
    w_self,
    w_neigh,
    sems,
):
    i = pl.program_id(0)
    v_blocks = feat.shape[0] // BLOCK
    b_blocks = bnd.shape[0] // BLOCK
    n_tiles = adj.shape[1] // BLOCK
    k_each = slots.shape[0]

    @pl.when(i == 0)
    def _():
        first = pltpu.make_async_copy(w_self_hbm, w_self, sems.at[0])
        second = pltpu.make_async_copy(w_neigh_hbm, w_neigh, sems.at[1])
        first.start()
        second.start()

        @pl.loop(0, v_blocks // 8)
        def _(c):
            for u in range(8):
                e = c * 8 + u
                ext_t[e] = feat[pl.ds(pl.multiple_of(e * BLOCK, BLOCK), BLOCK), :].T
                dext[e] = jnp.zeros((BLOCK, BLOCK), F32)

        for u in range(b_blocks):
            ext_t[v_blocks + u] = bnd[u * BLOCK : (u + 1) * BLOCK, :].T
            dext[v_blocks + u] = jnp.zeros((BLOCK, BLOCK), F32)
        gw[...] = jnp.zeros_like(gw)
        first.wait()
        second.wait()
        wt[:, :BLOCK] = w_self[...].T
        wt[:, BLOCK:] = w_neigh[...].T
        used = wct_raw.shape[0]
        padded = jnp.concatenate(
            [wct_raw[...].astype(F32), jnp.zeros((BLOCK - used, BLOCK), F32)], axis=0
        )
        half = wct.shape[0]
        wct[...] = padded[:half, :].astype(BF)
        side = padded.T[:, :half].astype(BF)
        wc2[:, :half] = side
        wc2[:, half:] = side
        bias[...] = jnp.broadcast_to(bias_row[...], (BLOCK, BLOCK)).T
        gcls[...] = jnp.zeros_like(gcls)
        gbias[...] = jnp.zeros_like(gbias)
        low = rows[...] & (BLOCK - 1)
        high = (rows[...] >> 7).astype(F32)
        within = lax.broadcasted_iota(jnp.int32, marks.shape, 0)
        marks[...] = jnp.where(within == low, high, -1.0).astype(BF)

    row_id = lax.broadcasted_iota(jnp.int32, (BLOCK, BLOCK), 0)
    for j in range(STEP_BLOCKS):
        lanes = slice(j * BLOCK, (j + 1) * BLOCK)
        q = slots[:, lanes]
        low = q & (BLOCK - 1)
        weight = jnp.left_shift(jnp.ones_like(q), (q >> 7) * 4)
        digits = jnp.zeros((BLOCK, BLOCK), jnp.int32)
        for k in range(k_each):
            digits += jnp.where(row_id == low[k : k + 1, :], weight[k : k + 1, :], 0)
        total = jnp.zeros((BLOCK, BLOCK), F32)
        for t in range(n_tiles):
            count = ((digits >> (4 * t)) & 15).astype(F32).astype(BF)
            adj[j, t * BLOCK : (t + 1) * BLOCK, :] = count
        slab = jnp.concatenate(
            [ext_t[tiles[t, i * STEP_BLOCKS + j]] for t in range(n_tiles)], axis=1
        )
        total = dot(slab, adj[j])
        xt[:BLOCK, lanes] = ext_t[i * STEP_BLOCKS + j]
        xt[BLOCK:, lanes] = (total * (1.0 / k_each)).astype(BF)

    class_id = lax.broadcasted_iota(jnp.int32, (wct.shape[0], SUB), 0)
    subs = [slice(s * SUB, (s + 1) * SUB) for s in range(STEP_BLOCKS * BLOCK // SUB)]
    wide_bias = jnp.concatenate([bias[...]] * (SUB // BLOCK), axis=1)
    pres = [dot(wt[...], xt[:, lanes]) + wide_bias for lanes in subs]
    sigmas = [1.0 / (1.0 + jnp.exp(-pre)) for pre in pres]
    hiddens = [(pre * sigma).astype(BF) for pre, sigma in zip(pres, sigmas)]
    slopes = [sigma * (1.0 + pre * (1.0 - sigma)) for pre, sigma in zip(pres, sigmas)]
    logits = [dot(wct[...], hidden) for hidden in hiddens]
    expos = [jnp.where(class_id < classes, jnp.exp(one), 0.0) for one in logits]
    dlogs = [
        expo / jnp.sum(expo, axis=0, keepdims=True)
        - jnp.where(class_id == labels[:, lanes], 1.0, 0.0)
        for expo, lanes in zip(expos, subs)
    ]
    d_his = [dlog.astype(BF) for dlog in dlogs]
    d_twos = [
        jnp.concatenate([d_hi, (dlog - d_hi.astype(F32)).astype(BF)], axis=0)
        for dlog, d_hi in zip(dlogs, d_his)
    ]
    dpres = [dot(wc2[...], d2) * slope for d2, slope in zip(d_twos, slopes)]
    gbias[...] += sum(
        dpre[:, u * BLOCK : (u + 1) * BLOCK] for dpre in dpres for u in range(SUB // BLOCK)
    )
    dpb = jnp.concatenate([dpre.astype(BF).T for dpre in dpres], axis=0)
    gcls[...] += dot(
        jnp.concatenate(hiddens, axis=1), jnp.concatenate([d2.T for d2 in d_twos], axis=0)
    )
    gw[...] += dot(xt[...], dpb)
    both = dot(dpb, wt[...])
    dmeans = both[:, BLOCK:].astype(BF) * BF(1.0 / k_each)
    for u in range(STEP_BLOCKS):
        b = i * STEP_BLOCKS + u
        spread = jnp.where(
            marks[...] == (jnp.zeros((1, 1), jnp.int32) + b).astype(F32).astype(BF), BF(1), BF(0)
        )
        dext[b] += both[u * BLOCK : (u + 1) * BLOCK, :BLOCK] + dot(spread, back[...])

    for j in range(STEP_BLOCKS):
        dslab = dot(adj[j], dmeans[j * BLOCK : (j + 1) * BLOCK, :])
        for t in range(n_tiles):
            e = tiles[t, i * STEP_BLOCKS + j]
            dext[e] += dslab[t * BLOCK : (t + 1) * BLOCK, :]

    @pl.when(i == pl.num_programs(0) - 1)
    def _():
        own = pltpu.make_async_copy(dext.at[pl.ds(0, v_blocks)], out_g, sems.at[0])
        halo = pltpu.make_async_copy(dext.at[pl.ds(v_blocks, b_blocks)], out_h, sems.at[1])
        own.start()
        halo.start()
        n_w = gw.shape[0]
        half = gcls.shape[1] // 2
        by_class = gcls[...].T
        out_w[:n_w, :] = gw[...]
        out_w[n_w : n_w + half, :] = by_class[:half, :] + by_class[half:, :]
        out_w[n_w + half : n_w + half + 8, :] = jnp.broadcast_to(
            jnp.sum(gbias[...].T, axis=0, keepdims=True), (8, BLOCK)
        )
        out_w[n_w + half + 8 :, :] = jnp.zeros((out_w.shape[0] - n_w - half - 8, BLOCK), F32)
        own.wait()
        halo.wait()


def layer(n, features, boundary, back, rows, tiles, slots, labels, w_self, w_neigh, bias, wct):
    v_dev, width = features.shape
    v_blocks = v_dev // BLOCK
    b_blocks = boundary.shape[0] // BLOCK
    n_tiles = tiles.shape[0]
    classes = wct.shape[0]
    half = -(-classes // 16) * 16
    grid = v_blocks // STEP_BLOCKS
    chunk = STEP_BLOCKS * BLOCK
    used = 2 * width + half + 8
    unit = 8 * n
    w_rows = -(-used // unit) * unit

    def whole(array):
        return pl.BlockSpec(array.shape, lambda i: (0,) * array.ndim)

    return pl.pallas_call(
        functools.partial(layer_kernel, classes),
        grid=(grid,),
        out_shape=(
            jax.ShapeDtypeStruct((v_blocks, BLOCK, width), F32),
            jax.ShapeDtypeStruct((b_blocks, BLOCK, width), F32),
            jax.ShapeDtypeStruct((w_rows, width), F32),
        ),
        in_specs=[
            pl.BlockSpec(memory_space=pltpu.SMEM),
            whole(features),
            whole(boundary),
            whole(back),
            whole(rows),
            pl.BlockSpec((slots.shape[0], chunk), lambda i: (0, i)),
            pl.BlockSpec((1, chunk), lambda i: (0, i)),
            pl.BlockSpec(memory_space=pl.ANY),
            pl.BlockSpec(memory_space=pl.ANY),
            whole(bias),
            whole(wct),
        ],
        out_specs=(
            pl.BlockSpec(memory_space=pl.ANY),
            pl.BlockSpec(memory_space=pl.ANY),
            pl.BlockSpec((w_rows, width), lambda i: (0, 0)),
        ),
        scratch_shapes=[
            pltpu.VMEM((v_blocks + b_blocks, width, BLOCK), BF),
            pltpu.VMEM((v_blocks + b_blocks, BLOCK, width), F32),
            pltpu.VMEM((STEP_BLOCKS, n_tiles * BLOCK, BLOCK), BF),
            pltpu.VMEM((2 * width, chunk), BF),
            pltpu.VMEM((BLOCK, rows.shape[1]), BF),
            pltpu.VMEM((2 * width, width), F32),
            pltpu.VMEM((width, 2 * half), F32),
            pltpu.VMEM((width, BLOCK), F32),
            pltpu.VMEM((width, 2 * width), BF),
            pltpu.VMEM((half, width), BF),
            pltpu.VMEM((width, 2 * half), BF),
            pltpu.VMEM((width, BLOCK), F32),
            pltpu.VMEM(w_self.shape, BF),
            pltpu.VMEM(w_neigh.shape, BF),
            pltpu.SemaphoreType.DMA((2,)),
        ],
        compiler_params=pltpu.CompilerParams(
            dimension_semantics=("arbitrary",), vmem_limit_bytes=58 * 1024 * 1024
        ),
        name="layer",
    )(tiles, features, boundary, back, rows, slots, labels, w_self, w_neigh, bias, wct)


def reduce_kernel(n, near, scale, src, out, buf1, buf2, acc, mine, sem):
    me = lax.axis_index("dom")
    far = n // near
    a = lax.rem(me, near)
    z = lax.div(me, near)
    wide = src.shape[0] // near
    narrow = wide // far

    def near_id(d):
        return lax.rem(a + d, near)

    def far_id(d):
        return lax.rem(z + d, far)

    barrier = pltpu.get_barrier_semaphore()
    for d in range(1, near):
        pl.semaphore_signal(barrier, inc=1, device_id={"dom": z * near + near_id(d)})
    for d in range(1, far):
        pl.semaphore_signal(barrier, inc=1, device_id={"dom": far_id(d) * near + a})
    pl.semaphore_wait(barrier, near + far - 2)

    def rows(start, size):
        return pl.ds(pl.multiple_of(start, 8), size)

    def send(src_ref, dst_ref, slot, device):
        return pltpu.make_async_remote_copy(
            src_ref=src_ref,
            dst_ref=dst_ref,
            send_sem=sem.at[0, slot],
            recv_sem=sem.at[1, slot],
            device_id={"dom": device},
        )

    def run(copies):
        for c in copies:
            c.start()
        for c in copies:
            c.wait()

    run(
        [
            send(src.at[rows(near_id(d) * wide, wide)], buf1.at[d - 1], d - 1, z * near + near_id(d))
            for d in range(1, near)
        ]
    )
    part = src[rows(a * wide, wide), :]
    for d in range(1, near):
        part += buf1[d - 1]
    acc[...] = part
    base = near - 1
    run(
        [
            send(
                acc.at[rows(far_id(d) * narrow, narrow)],
                buf2.at[d - 1],
                base + d - 1,
                far_id(d) * near + a,
            )
            for d in range(1, far)
        ]
    )
    part = acc[rows(z * narrow, narrow), :]
    for d in range(1, far):
        part += buf2[d - 1]
    own = rows(a * wide + z * narrow, narrow)
    mine[...] = part * scale
    out[own, :] = part * scale
    base += far - 1
    run(
        [
            send(mine, out.at[own], base + d - 1, far_id(d) * near + a)
            for d in range(1, far)
        ]
    )
    base += far - 1
    full = rows(a * wide, wide)
    run(
        [
            send(out.at[full], out.at[full], base + d - 1, z * near + near_id(d))
            for d in range(1, near)
        ]
    )


def reduce_all(n, partial, scale):
    near = 4 if n % 4 == 0 else n
    far = n // near
    wide = partial.shape[0] // near
    width = partial.shape[1]
    vmem = pl.BlockSpec(memory_space=pltpu.VMEM)
    return pl.pallas_call(
        functools.partial(reduce_kernel, n, near, scale),
        out_shape=jax.ShapeDtypeStruct(partial.shape, F32),
        in_specs=[vmem],
        out_specs=vmem,
        scratch_shapes=[
            pltpu.VMEM((near - 1, wide, width), F32),
            pltpu.VMEM((max(far - 1, 1), wide // far, width), F32),
            pltpu.VMEM((wide, width), F32),
            pltpu.VMEM((wide // far, width), F32),
            pltpu.SemaphoreType.DMA((2, 2 * (near + far - 2))),
        ],
        compiler_params=pltpu.CompilerParams(collective_id=1, has_side_effects=True),
        name="reduce",
    )(partial)


def finish_kernel(total, w_self, w_neigh, shift, by_class):
    width = w_self.shape[0]
    classes = by_class.shape[0]
    half = -(-classes // 16) * 16
    w_self[...] = total[:width, :]
    w_neigh[...] = total[width : 2 * width, :]
    by_class[...] = total[2 * width : 2 * width + classes, :]
    shift[...] = total[2 * width + half : 2 * width + half + 1, :]


def finish(total, classes):
    width = total.shape[1]
    square = jax.ShapeDtypeStruct((width, width), F32)
    w_self, w_neigh, shift, by_class = pl.pallas_call(
        finish_kernel,
        out_shape=(
            square,
            square,
            jax.ShapeDtypeStruct((1, width), F32),
            jax.ShapeDtypeStruct((classes, width), F32),
        ),
        name="finish",
    )(total)
    return w_self, w_neigh, shift.reshape(-1), by_class.T


def run_layer_raw(
    n, features, boundary, back, rows, tb, slots, labels, w_self, w_neigh, bias, w_cls
):
    return layer(
        n,
        features,
        boundary,
        back,
        rows.reshape(1, -1),
        tb.T,
        slots.T,
        labels.reshape(1, -1),
        w_self,
        w_neigh,
        bias.reshape(1, -1),
        w_cls.T,
    )


def run_layer(n, *args):
    width = args[0].shape[1]
    classes = args[-1].shape[1]
    grad, halo, total = run_layer_raw(n, *args)
    return (
        grad.reshape(-1, width),
        halo.reshape(-1, width),
        total[:width],
        total[width : 2 * width],
        total[2 * width + 16],
        total[2 * width : 2 * width + classes].T,
    )


def body(
    n,
    features,
    stale_features,
    stale_grads,
    send_rows,
    send_count,
    tile_block,
    neighbor_slot,
    labels,
    w_self,
    w_neigh,
    bias,
    w_cls,
):
    v_dev, width = features.shape
    classes = w_cls.shape[1]
    boundary, back, rows = exchange(
        n, send_count, send_rows, stale_features, stale_grads.reshape(send_rows.shape + (width,))
    )
    grad, halo, partial = run_layer_raw(
        n,
        features,
        boundary.reshape(-1, width),
        back.reshape(-1, width),
        rows,
        tile_block,
        neighbor_slot,
        labels,
        w_self,
        w_neigh,
        bias,
        w_cls,
    )
    scale = 1.0 / math.sqrt(v_dev * n)
    total = reduce_all(n, partial, scale)
    return (
        grad.reshape(v_dev, width),
        halo.reshape(-1, width),
        *finish(total, w_cls.shape[1]),
    )


def solution(mesh):
    split = P(("groups", "dom"), None)
    placed = (split,) * 7 + (P(("groups", "dom")),) + (P(),) * 4
    return jax.shard_map(
        functools.partial(body, mesh.shape["dom"]),
        mesh=mesh,
        in_specs=placed,
        out_specs=(
            split,
            split,
            P("groups", None),
            P("groups", None),
            P("groups"),
            P("groups", None),
        ),
        check_vma=False,
    )
```
